32 devices in a mesh: loop: 2 (over core), dp: 16 (over z, y, x).
Axes of the slice: x: 2, y: 2, z: 4, core: 2. Of those that a mesh axis runs over, the one named last changes fastest.
Arguments:
- tokens: bfloat16 [4096, 4096], P('dp', 'loop'), may hold values from -6 to 6
- probs: float32 [4096, 2], P('dp'), may hold values from 0.05 to 1
- routes: int32 [4096, 2], P('dp'), may hold values from 0 to 15, all different within a row; in each aligned block of 256 rows (0 to 255, 256 to 511, ...) at most 48 rows name the same one
- out_grad: bfloat16 [4096, 4096], P('dp', 'loop'), may hold values from -6 to 6
- w_gate: bfloat16 [16, 1536, 4096], P('dp', 'loop'), may hold values from -0.09375 to 0.09375
- w_up: bfloat16 [16, 1536, 4096], P('dp', 'loop'), may hold values from -0.09375 to 0.09375
- w_down: bfloat16 [16, 1536, 4096], P('dp', 'loop'), may hold values from -0.15625 to 0.15625
Outputs:
- layer_out: bfloat16 [4096, 4096], P('dp', 'loop')
- input_grad: bfloat16 [4096, 4096], P('dp', 'loop')
- prob_grad: float32 [4096, 2], P('dp')
- grad_gate: bfloat16 [16, 1536, 4096], P('dp', 'loop')
- grad_up: bfloat16 [16, 1536, 4096], P('dp', 'loop')
- grad_down: bfloat16 [16, 1536, 4096], P('dp', 'loop')
The draws below stay inside these ranges and needn't reach their ends.
Inputs may be any that keep to these rules, and one draw needn't show every extreme that they name: `routes`: A token's 2 experts differ. Among the 256 tokens of one dp index no expert is named more than 48 times, and in every draw some expert is named exactly 48 times there.
All inputs are finite; a program needn't handle non-finite values.
Results may differ from the reference program's by a relative error of at most 0.0072.
Values may be sent and summed in bfloat16 or wider, within the bound.
A program may use at most 192 MiB of HBM per device.

```python
import math
import jax
import jax.numpy as jnp
import numpy as np
from jax import lax

D = 4096
FF = 1536
TOK_DEV = 256
TOPK = 2
EXPERTS = 16
TOKENS = 4096
CAP = 48
N_LOOP = 2
N_DP = 16


def block_levels(own_key, dims, shards, low, high):
    def one(dim, shards_of):
        steps = jax.random.uniform(jax.random.fold_in(jax.random.fold_in(own_key, 6), dim), (shards_of,), jnp.float32, low / len(shards), high / len(shards))
        return jnp.repeat(jnp.exp(steps), dims[dim] // shards_of).reshape((-1,) + (1,) * (len(dims) - dim - 1))

    gain = one(*shards[0])
    for cut in shards[1:]:
        gain = gain * one(*cut)
    return gain


def routed_block(stream_key, own, number, rows, number_of, top, limit, lean):
    order = jax.random.permutation(stream_key, number_of)
    heavy_load, common = shares(number_of, rows * top, limit, lean, True), shares(number_of, rows * top, limit, lean, False)
    places = jnp.arange(number_of)

    def named(lengths, turn):
        used = int((lengths > 0).sum())
        fixed = max(1, used // 4)
        shifted = fixed + (places - fixed + turn * (used - fixed)) % max(1, number_of - fixed)
        return jnp.zeros((number_of,), jnp.int32).at[order[jnp.where(places < fixed, places, shifted)]].set(jnp.asarray(lengths, jnp.int32))

    lengths = jnp.where(number % 4 == 0, named(heavy_load, number // 4), named(common, number - number // 4 - 1))
    mixed = jax.random.permutation(jax.random.fold_in(own, 3), number_of)
    giver, receiver = mixed[0:number_of // 2 * 2:2], mixed[1:number_of // 2 * 2:2]
    margin = jnp.minimum(lengths[giver] - 1, limit - lengths[receiver]) // 2
    margin = jnp.where((giver == order[0]) | (receiver == order[0]) | (lengths[receiver] == 0), 0, jnp.maximum(margin, 0))
    shifted = jax.random.randint(jax.random.fold_in(own, 4), (number_of // 2,), 0, 1 << 20) % (margin + 1)
    lengths = lengths.at[giver].add(-shifted).at[receiver].add(shifted)
    members = jnp.searchsorted(jnp.cumsum(lengths), jnp.arange(rows * top), side="right").astype(jnp.int32)
    table = members.reshape(top, rows).T
    table = table[jax.random.permutation(jax.random.fold_in(own, 1), rows)]
    turn = jax.random.randint(jax.random.fold_in(own, 2), (rows, 1), 0, top)
    return jnp.take_along_axis(table, (jnp.arange(top)[None, :] + turn) % top, axis=1)


def shares(amount, total, limit, slope, full):
    weights = [(1 << 20) // math.isqrt(rank ** slope) + 1 for rank in range(1, amount + 1)]
    largest = limit if full else min(limit, max(-(-total // amount), total * weights[0] // sum(weights)))
    least = 1 if total - largest >= amount - 1 else 0
    given, rest = [largest] + [least] * (amount - 1), total - largest - least * (amount - 1)
    while rest > 0:
        free = [i for i in range(1, amount) if given[i] < largest] or [i for i in range(1, amount) if given[i] < limit]
        pool, budget = sum([weights[i] for i in free]), rest
        for i in free:
            extra = min(limit - given[i], max(1, budget * weights[i] // pool), rest)
            given[i] = given[i] + extra
            rest = rest - extra
    return np.array(given)


def noise(stream_key, dims, deviation, reach, pieces=(), kind=jnp.bfloat16):
    result = deviation * jax.random.normal(stream_key, dims, jnp.float32)
    if pieces:
        result = result * block_levels(stream_key, dims, pieces, -0.22, 0.18)
    return jnp.clip(result, -reach, reach).astype(kind)


def setup_inputs(seed: int = 0) -> dict:
    key_of = jax.random.split(jax.random.key(seed), 8)
    tokens = noise(key_of[0], (TOKENS, D), 1.0, 6.0, ((0, 16), (1, 2)))
    probs = jnp.clip(jnp.exp(math.log(1.0) - 2.9957323 * jax.random.uniform(key_of[1], (TOKENS, TOPK), jnp.float32) ** block_levels(key_of[1], (TOKENS, TOPK), ((0, 16),), -0.2, 0.2)), 0.05, 1.0)
    routes_keys = jax.random.split(jax.random.fold_in(key_of[2], 1), TOKENS // TOK_DEV)
    routes_turns = jax.random.permutation(jax.random.fold_in(key_of[2], 3), TOKENS // TOK_DEV)
    routes = jax.vmap(lambda own, number: routed_block(jax.random.fold_in(key_of[2], 2), own, number, TOK_DEV, EXPERTS, TOPK, CAP, 2))(routes_keys, routes_turns).reshape((TOKENS, TOPK))
    out_grad = noise(key_of[3], (TOKENS, D), 1.0, 6.0, ((0, 16), (1, 2)))
    w_gate = noise(key_of[4], (EXPERTS, FF, D), D ** -0.5, 0.09375, ((0, 16), (1, 2)))
    w_up = noise(key_of[5], (EXPERTS, FF, D), D ** -0.5, 0.09375, ((0, 16), (1, 2)))
    w_down = noise(key_of[6], (EXPERTS, FF, D), FF ** -0.5, 0.15625, ((0, 16), (1, 2)))
    return {"tokens": tokens, "probs": probs, "routes": routes, "out_grad": out_grad, "w_gate": w_gate, "w_up": w_up, "w_down": w_down}


def slot_index(routes):
    blocks = routes.reshape(N_DP, TOK_DEV * TOPK).astype(jnp.int32)
    labels = jnp.arange(EXPERTS, dtype=jnp.int32)
    onehot = (blocks[:, :, None] == labels[None, None, :]).astype(jnp.int32)
    before = jnp.cumsum(onehot, axis=1) - onehot
    slot = jnp.sum(before * onehot, axis=2).astype(jnp.int32)
    source = jnp.arange(N_DP, dtype=jnp.int32)[:, None]
    index = blocks * (N_DP * CAP) + source * CAP + slot
    return index.reshape(-1).astype(jnp.int32)


def grouped(left, weight):
    rows = left.shape[0]
    left_groups = left.reshape(rows, N_LOOP, FF // N_LOOP).astype(jnp.float32)
    weight_groups = weight.reshape(N_LOOP, FF // N_LOOP, D).astype(jnp.float32)
    return jnp.einsum("rgf,gfd->grd", left_groups, weight_groups)


def round_groups(parts):
    rounded = lax.optimization_barrier(parts.astype(jnp.bfloat16))
    return jnp.sum(rounded.astype(jnp.float32), axis=0).astype(jnp.bfloat16)


def expert_step(operands):
    rows_x, rows_g, wg, wu, wd = operands
    contract = (((1,), (1,)), ((), ()))
    gate = lax.dot_general(rows_x, wg, contract, preferred_element_type=jnp.float32)
    up = lax.dot_general(rows_x, wu, contract, preferred_element_type=jnp.float32)
    sig = jax.nn.sigmoid(gate)
    silu = gate * sig
    hidden = (silu * up).astype(jnp.bfloat16)
    expert_out = round_groups(grouped(hidden, wd))
    dhid = lax.dot_general(rows_g, wd, contract, preferred_element_type=jnp.float32)
    dgate = (dhid * up * sig * (1.0 + gate * (1.0 - sig))).astype(jnp.bfloat16)
    dup = (dhid * silu).astype(jnp.bfloat16)
    expert_dx = round_groups(grouped(dgate, wg) + grouped(dup, wu))
    outer = (((0,), (0,)), ((), ()))
    grad_g = lax.dot_general(dgate, rows_x, outer, preferred_element_type=jnp.float32).astype(jnp.bfloat16)
    grad_u = lax.dot_general(dup, rows_x, outer, preferred_element_type=jnp.float32).astype(jnp.bfloat16)
    grad_d = lax.dot_general(hidden, rows_g, outer, preferred_element_type=jnp.float32).astype(jnp.bfloat16)
    return expert_out, expert_dx, grad_g, grad_u, grad_d


def reference(tokens, probs, routes, out_grad, w_gate, w_up, w_down):
    index = slot_index(routes)
    total_rows = N_DP * CAP
    copies = jnp.repeat(tokens, TOPK, axis=0)
    scaled = (probs[:, :, None] * out_grad[:, None, :].astype(jnp.float32)).astype(jnp.bfloat16).reshape(-1, D)
    buffer_x = jnp.zeros((EXPERTS * total_rows, D), jnp.bfloat16).at[index].set(copies).reshape(EXPERTS, total_rows, D)
    buffer_g = jnp.zeros((EXPERTS * total_rows, D), jnp.bfloat16).at[index].set(scaled).reshape(EXPERTS, total_rows, D)
    expert_out, expert_dx, grad_gate, grad_up, grad_down = lax.map(expert_step, (buffer_x, buffer_g, w_gate, w_up, w_down))
    out_rows = expert_out.reshape(-1, D)[index].reshape(TOKENS, TOPK, D).astype(jnp.float32)
    dx_rows = expert_dx.reshape(-1, D)[index].reshape(TOKENS, TOPK, D).astype(jnp.float32)
    layer_out = jnp.sum(probs[:, :, None] * out_rows, axis=1).astype(jnp.bfloat16)
    input_grad = jnp.sum(dx_rows, axis=1).astype(jnp.bfloat16)
    prob_grad = jnp.sum(out_grad.astype(jnp.float32)[:, None, :] * out_rows, axis=2)
    return layer_out, input_grad, prob_grad, grad_gate, grad_up, grad_down
```

```python
import jax
import jax.numpy as jnp
from jax import lax
from jax.sharding import PartitionSpec as P


def shards(tokens, probs, routes, out_grad, w_gate, w_up, w_down):
    tok_count = tokens.shape[0]
    top_count = routes.shape[1]
    experts = lax.axis_size("dp")
    capacity = max(2, 3 * tok_count * top_count // (2 * experts))
    flat = routes.reshape(-1)
    count = flat.shape[0]
    labels = jnp.arange(experts, dtype=jnp.int32)
    onehot = flat[:, None] == labels[None, :]
    place = jnp.arange(count, dtype=jnp.int32)
    earlier = (place[None, :] < place[:, None]).astype(jnp.bfloat16)
    before = jnp.dot(earlier, onehot.astype(jnp.bfloat16), preferred_element_type=jnp.float32)
    rank = jnp.sum(jnp.where(onehot, before, 0.0), axis=1).astype(jnp.int32)
    target = (flat * capacity + rank).reshape(tok_count, top_count)
    slots = jnp.arange(experts * capacity, dtype=jnp.int32)
    picks = [slots[:, None] == target[:, k][None, :] for k in range(top_count)]
    pick = sum(p.astype(jnp.bfloat16) for p in picks)
    slot_prob = sum(
        jnp.sum(jnp.where(picks[k], probs[:, k][None, :], 0.0), axis=1) for k in range(top_count)
    )
    send_x = jnp.dot(pick, tokens, preferred_element_type=jnp.float32).astype(jnp.bfloat16)
    send_g = (
        jnp.dot(pick, out_grad, preferred_element_type=jnp.float32) * slot_prob[:, None]
    ).astype(jnp.bfloat16)

    def exchange(rows):
        cut = rows.reshape(experts, capacity, rows.shape[-1])
        moved = lax.all_to_all(cut, "dp", split_axis=0, concat_axis=0, tiled=True)
        return moved.reshape(experts * capacity, rows.shape[-1])

    part_x = exchange(send_x)
    part_x, send_g = lax.optimization_barrier((part_x, send_g))
    part_g = exchange(send_g)
    rows_x = lax.all_gather(part_x, "loop", axis=1, tiled=True)
    rows_g = lax.all_gather(part_g, "loop", axis=1, tiled=True)
    gate_rows = w_gate[0]
    up_rows = w_up[0]
    down_rows = w_down[0]
    contract = (((1,), (1,)), ((), ()))
    gate = lax.dot_general(rows_x, gate_rows, contract, preferred_element_type=jnp.float32)
    up = lax.dot_general(rows_x, up_rows, contract, preferred_element_type=jnp.float32)
    sig = jax.nn.sigmoid(gate)
    silu = gate * sig
    hidden = (silu * up).astype(jnp.bfloat16)
    out_part = jnp.dot(hidden, down_rows, preferred_element_type=jnp.float32)
    dhid = lax.dot_general(rows_g, down_rows, contract, preferred_element_type=jnp.float32)
    dgate = (dhid * up * sig * (1.0 + gate * (1.0 - sig))).astype(jnp.bfloat16)
    dup = (dhid * silu).astype(jnp.bfloat16)
    dx_part = jnp.dot(dgate, gate_rows, preferred_element_type=jnp.float32) + jnp.dot(
        dup, up_rows, preferred_element_type=jnp.float32
    )
    outer = (((0,), (0,)), ((), ()))
    grad_gate = lax.dot_general(dgate, rows_x, outer, preferred_element_type=jnp.float32).astype(
        jnp.bfloat16
    )[None]
    grad_up = lax.dot_general(dup, rows_x, outer, preferred_element_type=jnp.float32).astype(
        jnp.bfloat16
    )[None]
    grad_down = lax.dot_general(hidden, rows_g, outer, preferred_element_type=jnp.float32).astype(
        jnp.bfloat16
    )[None]
    out_sum = lax.psum_scatter(
        out_part.astype(jnp.bfloat16), "loop", scatter_dimension=1, tiled=True
    )
    back_out = exchange(out_sum)
    dx_sum = lax.psum_scatter(
        dx_part.astype(jnp.bfloat16), "loop", scatter_dimension=1, tiled=True
    )
    back_out, dx_sum = lax.optimization_barrier((back_out, dx_sum))
    back_dx = exchange(dx_sum)
    wanted = [(target[:, k][:, None] == slots[None, :]) for k in range(top_count)]
    out_rows = [
        jnp.dot(w.astype(jnp.bfloat16), back_out, preferred_element_type=jnp.float32)
        for w in wanted
    ]
    layer_out = sum(probs[:, k][:, None] * out_rows[k] for k in range(top_count)).astype(
        jnp.bfloat16
    )
    grad32 = out_grad.astype(jnp.float32)
    partial_dots = jnp.stack([jnp.sum(grad32 * rows, axis=1) for rows in out_rows], axis=1)
    prob_grad = lax.psum(partial_dots, "loop")
    both = sum(w.astype(jnp.bfloat16) for w in wanted)
    input_grad = jnp.dot(both, back_dx, preferred_element_type=jnp.float32).astype(jnp.bfloat16)
    return (layer_out, input_grad, prob_grad, grad_gate, grad_up, grad_down)


def solution(mesh):
    in_specs = (
        P("dp", "loop"),
        P("dp", None),
        P("dp", None),
        P("dp", "loop"),
        P("dp", "loop", None),
        P("dp", "loop", None),
        P("dp", "loop", None),
    )
    out_specs = (
        P("dp", "loop"),
        P("dp", "loop"),
        P("dp", None),
        P("dp", "loop", None),
        P("dp", "loop", None),
        P("dp", "loop", None),
    )
    return jax.shard_map(shards, mesh=mesh, in_specs=in_specs, out_specs=out_specs, check_vma=False)
```

```python
import functools

import jax
import jax.numpy as jnp
from jax import lax
from jax.experimental import pallas as pl
from jax.experimental.pallas import tpu as pltpu
from jax.sharding import PartitionSpec as P

BF = jnp.bfloat16
F32 = jnp.float32
CONTRACT = (((1,), (1,)), ((), ()))
STEP = 256
WIDE = 512


def middle(
    n, send_x, send_g, w_gate, w_up, w_down,
    full_x, full_g, hidden, dgate, dup, back_out, dx_sum,
    wg, wu, wd, fact_gate, fact_up, out_own, to_mate, mate_out, mate_dx,
    x_out, x_in, xm_out, xm_in, g_out, g_in, gm_out, gm_in, o_out, o_in,
    mate_send, mate_recv, local_sem,
):
    me = lax.axis_index("dp")
    side = lax.axis_index("loop")
    mate = 1 - side
    cap, part = send_x.shape[1:]
    rows = n * cap
    units = wg.shape[0]
    mine = pl.ds(pl.multiple_of(side * part, part), part)

    def peer(step):
        return lax.rem(me + step, n)

    def source(step):
        return lax.rem(me - step + n, n)

    def over_dp(src, dst, out_sem, in_sem, step):
        return pltpu.make_async_remote_copy(
            src_ref=src, dst_ref=dst, send_sem=out_sem.at[step], recv_sem=in_sem.at[step],
            device_id={"dp": peer(step)}, device_id_type=pl.DeviceIdType.MESH,
        )

    def over_loop(src, dst, out_sem, in_sem, step):
        return pltpu.make_async_remote_copy(
            src_ref=src, dst_ref=dst, send_sem=out_sem.at[step], recv_sem=in_sem.at[step],
            device_id={"loop": mate}, device_id_type=pl.DeviceIdType.MESH,
        )

    def x_copy(step):
        return over_dp(send_x.at[peer(step)], full_x.at[me, :, mine], x_out, x_in, step)

    def g_copy(step):
        return over_dp(send_g.at[peer(step)], full_g.at[me, :, mine], g_out, g_in, step)

    def o_copy(step):
        return over_dp(out_own.at[peer(step)], back_out.at[me], o_out, o_in, step)

    def handed(full, step, out_sem, in_sem):
        at = full.at[source(step), :, mine]
        return over_loop(at, at, out_sem, in_sem, step)

    barrier = pltpu.get_barrier_semaphore()

    @pl.loop(1, n)
    def _(step):
        pl.semaphore_signal(
            barrier, inc=1, device_id={"dp": peer(step)}, device_id_type=pl.DeviceIdType.MESH
        )

    pl.semaphore_signal(
        barrier, inc=1, device_id={"loop": mate}, device_id_type=pl.DeviceIdType.MESH
    )
    pl.semaphore_wait(barrier, n)

    @pl.loop(1, n)
    def _(step):
        x_copy(step).start()

    own_x = pltpu.make_async_copy(send_x.at[me], full_x.at[me, :, mine], local_sem.at[0])
    own_g = pltpu.make_async_copy(send_g.at[me], full_g.at[me, :, mine], local_sem.at[1])
    weights = [
        pltpu.make_async_copy(src, dst, local_sem.at[2 + i])
        for i, (src, dst) in enumerate(((w_gate, wg), (w_up, wu), (w_down, wd)))
    ]
    own_x.start()
    own_g.start()
    for copy in weights:
        copy.start()
    own_x.wait()
    own_g.wait()
    handed(full_x, 0, xm_out, xm_in).start()
    handed(full_g, 0, gm_out, gm_in).start()

    @pl.loop(1, n)
    def _(step):
        x_copy(step).wait()
        handed(full_x, step, xm_out, xm_in).start()
        g_copy(step).start()

    for copy in weights:
        copy.wait()

    @pl.loop(0, n)
    def _(step):
        handed(full_x, step, xm_out, xm_in).wait()

    @pl.loop(0, units // STEP)
    def _(i):
        at = pl.ds(pl.multiple_of(i * STEP, STEP), STEP)
        x = full_x[...].reshape(rows, 2 * part)
        gate = lax.dot_general(x, wg[at, :], CONTRACT, preferred_element_type=F32)
        up = lax.dot_general(x, wu[at, :], CONTRACT, preferred_element_type=F32)
        sig = jax.nn.sigmoid(gate)
        silu = gate * sig
        hidden[:, at] = (silu * up).astype(BF)
        fact_up[:, at] = silu
        fact_gate[:, at] = up * sig * (1.0 + gate * (1.0 - sig))

    def fill(dst, which, product):
        @pl.loop(0, part // WIDE)
        def _(i):
            first = pl.multiple_of(i * WIDE, WIDE)
            at = pl.ds(pl.multiple_of(which * part + first, WIDE), WIDE)
            dst[:, :, pl.ds(first, WIDE)] = product(at).astype(BF).reshape(n, cap, WIDE)

    def add(dst, other):
        @pl.loop(0, n)
        def _(i):
            dst[i] = (dst[i].astype(F32) + other[i].astype(F32)).astype(BF)

    def out_product(at):
        return jnp.dot(hidden[...], wd[:, at], preferred_element_type=F32)

    fill(to_mate, mate, out_product)
    swap_out = over_loop(to_mate, mate_out, mate_send, mate_recv, 0)
    swap_out.start()
    fill(out_own, side, out_product)
    swap_out.wait()
    add(out_own, mate_out)

    @pl.loop(1, n)
    def _(step):
        g_copy(step).wait()
        handed(full_g, step, gm_out, gm_in).start()
        o_copy(step).start()

    own_out = pltpu.make_async_copy(out_own.at[me], back_out.at[me], local_sem.at[5])
    own_out.start()

    @pl.loop(0, n)
    def _(step):
        handed(full_g, step, gm_out, gm_in).wait()

    @pl.loop(0, units // STEP)
    def _(i):
        at = pl.ds(pl.multiple_of(i * STEP, STEP), STEP)
        g = full_g[...].reshape(rows, 2 * part)
        dhid = lax.dot_general(g, wd[at, :], CONTRACT, preferred_element_type=F32)
        dgate[:, at] = (dhid * fact_gate[:, at]).astype(BF)
        dup[:, at] = (dhid * fact_up[:, at]).astype(BF)

    def dx_product(at):
        return jnp.dot(dgate[...], wg[:, at], preferred_element_type=F32) + jnp.dot(
            dup[...], wu[:, at], preferred_element_type=F32
        )

    fill(to_mate, mate, dx_product)
    swap_dx = over_loop(to_mate, mate_dx, mate_send, mate_recv, 1)
    swap_dx.start()
    fill(dx_sum, side, dx_product)
    swap_dx.wait()
    add(dx_sum, mate_dx)
    own_out.wait()

    @pl.loop(1, n)
    def _(step):
        o_copy(step).wait()


def run_middle(send_x, send_g, w_gate, w_up, w_down):
    n, cap, part = send_x.shape
    units, width = w_gate.shape
    rows = n * cap
    vmem = pl.BlockSpec(memory_space=pltpu.VMEM)
    hbm = pl.BlockSpec(memory_space=pl.ANY)
    half = jax.ShapeDtypeStruct((n, cap, part), BF)
    full = jax.ShapeDtypeStruct((n, cap, width), BF)
    acts = jax.ShapeDtypeStruct((rows, units), BF)
    dma = pltpu.SemaphoreType.DMA
    return pl.pallas_call(
        functools.partial(middle, n),
        out_shape=(full, full, acts, acts, acts, half, half),
        in_specs=[hbm] * 5,
        out_specs=(vmem, vmem, vmem, vmem, vmem, hbm, vmem),
        scratch_shapes=[pltpu.VMEM((units, width), BF)] * 3
        + [pltpu.VMEM((rows, units), F32)] * 2
        + [pltpu.VMEM((n, cap, part), BF)] * 4
        + [dma((n,))] * 10
        + [dma((2,)), dma((2,)), dma((6,))],
        compiler_params=pltpu.CompilerParams(
            collective_id=0, has_side_effects=True, vmem_limit_bytes=61 * 1024 * 1024
        ),
        cost_estimate=pl.CostEstimate(
            flops=12 * rows * units * width, bytes_accessed=60_000_000, transcendentals=rows * units
        ),
    )(send_x, send_g, w_gate, w_up, w_down)


def shards(tokens, probs, routes, out_grad, w_gate, w_up, w_down):
    tok_count = tokens.shape[0]
    top_count = routes.shape[1]
    experts = lax.axis_size("dp")
    capacity = max(2, 3 * tok_count * top_count // (2 * experts))
    flat = routes.reshape(-1)
    count = flat.shape[0]
    labels = jnp.arange(experts, dtype=jnp.int32)
    onehot = flat[:, None] == labels[None, :]
    place = jnp.arange(count, dtype=jnp.int32)
    earlier = (place[None, :] < place[:, None]).astype(jnp.bfloat16)
    before = jnp.dot(earlier, onehot.astype(jnp.bfloat16), preferred_element_type=jnp.float32)
    rank = jnp.sum(jnp.where(onehot, before, 0.0), axis=1).astype(jnp.int32)
    target = (flat * capacity + rank).reshape(tok_count, top_count)
    slots = jnp.arange(experts * capacity, dtype=jnp.int32)
    picks = [slots[:, None] == target[:, k][None, :] for k in range(top_count)]
    pick = sum(p.astype(jnp.bfloat16) for p in picks)
    slot_prob = sum(
        jnp.sum(jnp.where(picks[k], probs[:, k][None, :], 0.0), axis=1) for k in range(top_count)
    )
    send_x = jnp.dot(pick, tokens, preferred_element_type=jnp.float32).astype(jnp.bfloat16)
    send_g = (
        jnp.dot(pick, out_grad, preferred_element_type=jnp.float32) * slot_prob[:, None]
    ).astype(jnp.bfloat16)

    def exchange(rows):
        cut = rows.reshape(experts, capacity, rows.shape[-1])
        moved = lax.all_to_all(cut, "dp", split_axis=0, concat_axis=0, tiled=True)
        return moved.reshape(experts * capacity, rows.shape[-1])

    if lax.axis_size("loop") == 2:
        shape = (experts, capacity, tokens.shape[1])
        rows_x, rows_g, hidden, dgate, dup, back_out, dx_sum = run_middle(
            send_x.reshape(shape), send_g.reshape(shape), w_gate[0], w_up[0], w_down[0]
        )
        rows_x = rows_x.reshape(experts * capacity, -1)
        rows_g = rows_g.reshape(experts * capacity, -1)
        back_out = back_out.reshape(experts * capacity, -1)
        dx_sum = dx_sum.reshape(experts * capacity, -1)
    else:
        part_x = exchange(send_x)
        part_x, send_g = lax.optimization_barrier((part_x, send_g))
        part_g = exchange(send_g)
        rows_x = lax.all_gather(part_x, "loop", axis=1, tiled=True)
        rows_g = lax.all_gather(part_g, "loop", axis=1, tiled=True)
        gate_rows = w_gate[0]
        up_rows = w_up[0]
        down_rows = w_down[0]
        contract = (((1,), (1,)), ((), ()))
        gate = lax.dot_general(rows_x, gate_rows, contract, preferred_element_type=jnp.float32)
        up = lax.dot_general(rows_x, up_rows, contract, preferred_element_type=jnp.float32)
        sig = jax.nn.sigmoid(gate)
        silu = gate * sig
        hidden = (silu * up).astype(jnp.bfloat16)
        out_part = jnp.dot(hidden, down_rows, preferred_element_type=jnp.float32)
        dhid = lax.dot_general(rows_g, down_rows, contract, preferred_element_type=jnp.float32)
        dgate = (dhid * up * sig * (1.0 + gate * (1.0 - sig))).astype(jnp.bfloat16)
        dup = (dhid * silu).astype(jnp.bfloat16)
        dx_part = jnp.dot(dgate, gate_rows, preferred_element_type=jnp.float32) + jnp.dot(
            dup, up_rows, preferred_element_type=jnp.float32
        )
        outs = lax.psum_scatter(out_part.astype(BF), "loop", scatter_dimension=1, tiled=True)
        back_out = exchange(outs)
        dx_sum = lax.psum_scatter(dx_part.astype(BF), "loop", scatter_dimension=1, tiled=True)
    back_dx = exchange(dx_sum)
    outer = (((0,), (0,)), ((), ()))
    grad_gate = lax.dot_general(dgate, rows_x, outer, preferred_element_type=jnp.float32).astype(
        jnp.bfloat16
    )[None]
    grad_up = lax.dot_general(dup, rows_x, outer, preferred_element_type=jnp.float32).astype(
        jnp.bfloat16
    )[None]
    grad_down = lax.dot_general(hidden, rows_g, outer, preferred_element_type=jnp.float32).astype(
        jnp.bfloat16
    )[None]
    wanted = [(target[:, k][:, None] == slots[None, :]) for k in range(top_count)]
    out_rows = [
        jnp.dot(w.astype(jnp.bfloat16), back_out, preferred_element_type=jnp.float32)
        for w in wanted
    ]
    layer_out = sum(probs[:, k][:, None] * out_rows[k] for k in range(top_count)).astype(
        jnp.bfloat16
    )
    grad32 = out_grad.astype(jnp.float32)
    partial_dots = jnp.stack([jnp.sum(grad32 * rows, axis=1) for rows in out_rows], axis=1)
    prob_grad = lax.psum(partial_dots, "loop")
    both = sum(w.astype(jnp.bfloat16) for w in wanted)
    input_grad = jnp.dot(both, back_dx, preferred_element_type=jnp.float32).astype(jnp.bfloat16)
    return (layer_out, input_grad, prob_grad, grad_gate, grad_up, grad_down)


def solution(mesh):
    in_specs = (
        P("dp", "loop"),
        P("dp", None),
        P("dp", None),
        P("dp", "loop"),
        P("dp", "loop", None),
        P("dp", "loop", None),
        P("dp", "loop", None),
    )
    out_specs = (
        P("dp", "loop"),
        P("dp", "loop"),
        P("dp", None),
        P("dp", "loop", None),
        P("dp", "loop", None),
        P("dp", "loop", None),
    )
    return jax.shard_map(shards, mesh=mesh, in_specs=in_specs, out_specs=out_specs, check_vma=False)
```

```python
import functools

import jax
import jax.numpy as jnp
from jax import lax
from jax.experimental import pallas as pl
from jax.experimental.pallas import tpu as pltpu
from jax.sharding import PartitionSpec as P

BF = jnp.bfloat16
F32 = jnp.float32
CONTRACT = (((1,), (1,)), ((), ()))
STEP = 256
WIDE = 512


def middle(
    n, send_x, send_g, w_gate, w_up, w_down,
    full_x, full_g, hidden, dgate, dup, back_out, dx_sum,
    wg, wu, wd, fact_gate, fact_up, out_own, to_mate, mate_out, mate_dx,
    x_out, x_in, xm_out, xm_in, g_out, g_in, gm_out, gm_in, o_out, o_in,
    mate_send, mate_recv, local_sem,
):
    me = lax.axis_index("dp")
    side = lax.axis_index("loop")
    mate = 1 - side
    cap, part = send_x.shape[1:]
    rows = n * cap
    units = wg.shape[0]
    ahead = n // 8
    mine = pl.ds(pl.multiple_of(side * part, part), part)

    def peer(step):
        return lax.rem(me + step, n)

    def source(step):
        return lax.rem(me - step + n, n)

    def over_dp(src, dst, out_sem, in_sem, step):
        return pltpu.make_async_remote_copy(
            src_ref=src, dst_ref=dst, send_sem=out_sem.at[step], recv_sem=in_sem.at[step],
            device_id={"dp": peer(step)}, device_id_type=pl.DeviceIdType.MESH,
        )

    def over_loop(src, dst, out_sem, in_sem, step):
        return pltpu.make_async_remote_copy(
            src_ref=src, dst_ref=dst, send_sem=out_sem.at[step], recv_sem=in_sem.at[step],
            device_id={"loop": mate}, device_id_type=pl.DeviceIdType.MESH,
        )

    def x_copy(step):
        return over_dp(send_x.at[peer(step)], full_x.at[me, :, mine], x_out, x_in, step)

    def g_copy(step):
        return over_dp(send_g.at[peer(step)], full_g.at[me, :, mine], g_out, g_in, step)

    def o_copy(step):
        return over_dp(out_own.at[peer(step)], back_out.at[me], o_out, o_in, step)

    def handed(full, step, out_sem, in_sem):
        at = full.at[source(step), :, mine]
        return over_loop(at, at, out_sem, in_sem, step)

    barrier = pltpu.get_barrier_semaphore()

    @pl.loop(1, n)
    def _(step):
        pl.semaphore_signal(
            barrier, inc=1, device_id={"dp": peer(step)}, device_id_type=pl.DeviceIdType.MESH
        )

    pl.semaphore_signal(
        barrier, inc=1, device_id={"loop": mate}, device_id_type=pl.DeviceIdType.MESH
    )
    pl.semaphore_wait(barrier, n)

    @pl.loop(1, n)
    def _(step):
        x_copy(step).start()

    @pl.loop(1, 1 + ahead)
    def _(step):
        g_copy(step).start()

    own_x = pltpu.make_async_copy(send_x.at[me], full_x.at[me, :, mine], local_sem.at[0])
    own_g = pltpu.make_async_copy(send_g.at[me], full_g.at[me, :, mine], local_sem.at[1])
    weights = [
        pltpu.make_async_copy(src, dst, local_sem.at[2 + i])
        for i, (src, dst) in enumerate(((w_gate, wg), (w_up, wu), (w_down, wd)))
    ]
    own_x.start()
    own_g.start()
    for copy in weights:
        copy.start()
    own_x.wait()
    own_g.wait()
    handed(full_x, 0, xm_out, xm_in).start()
    handed(full_g, 0, gm_out, gm_in).start()

    @pl.loop(1, n)
    def _(step):
        x_copy(step).wait()
        handed(full_x, step, xm_out, xm_in).start()

        @pl.when(step + ahead < n)
        def _():
            g_copy(step + ahead).start()

    for copy in weights:
        copy.wait()

    @pl.loop(0, n)
    def _(step):
        handed(full_x, step, xm_out, xm_in).wait()

    @pl.loop(0, units // STEP)
    def _(i):
        at = pl.ds(pl.multiple_of(i * STEP, STEP), STEP)
        x = full_x[...].reshape(rows, 2 * part)
        gate = lax.dot_general(x, wg[at, :], CONTRACT, preferred_element_type=F32)
        up = lax.dot_general(x, wu[at, :], CONTRACT, preferred_element_type=F32)
        sig = jax.nn.sigmoid(gate)
        silu = gate * sig
        hidden[:, at] = (silu * up).astype(BF)
        fact_up[:, at] = silu
        fact_gate[:, at] = up * sig * (1.0 + gate * (1.0 - sig))

    def fill(dst, which, product):
        @pl.loop(0, part // WIDE)
        def _(i):
            first = pl.multiple_of(i * WIDE, WIDE)
            at = pl.ds(pl.multiple_of(which * part + first, WIDE), WIDE)
            dst[:, :, pl.ds(first, WIDE)] = product(at).astype(BF).reshape(n, cap, WIDE)

    def add(dst, other):
        @pl.loop(0, n)
        def _(i):
            dst[i] = (dst[i].astype(F32) + other[i].astype(F32)).astype(BF)

    def out_product(at):
        return jnp.dot(hidden[...], wd[:, at], preferred_element_type=F32)

    fill(to_mate, mate, out_product)
    swap_out = over_loop(to_mate, mate_out, mate_send, mate_recv, 0)
    swap_out.start()
    fill(out_own, side, out_product)
    swap_out.wait()
    add(out_own, mate_out)

    @pl.loop(1, 1 + ahead)
    def _(step):
        o_copy(step).start()

    @pl.loop(1, n)
    def _(step):
        g_copy(step).wait()
        handed(full_g, step, gm_out, gm_in).start()

        @pl.when(step + ahead < n)
        def _():
            o_copy(step + ahead).start()

    own_out = pltpu.make_async_copy(out_own.at[me], back_out.at[me], local_sem.at[5])
    own_out.start()

    @pl.loop(0, n)
    def _(step):
        handed(full_g, step, gm_out, gm_in).wait()

    @pl.loop(0, units // STEP)
    def _(i):
        at = pl.ds(pl.multiple_of(i * STEP, STEP), STEP)
        g = full_g[...].reshape(rows, 2 * part)
        dhid = lax.dot_general(g, wd[at, :], CONTRACT, preferred_element_type=F32)
        dgate[:, at] = (dhid * fact_gate[:, at]).astype(BF)
        dup[:, at] = (dhid * fact_up[:, at]).astype(BF)

    def dx_product(at):
        return jnp.dot(dgate[...], wg[:, at], preferred_element_type=F32) + jnp.dot(
            dup[...], wu[:, at], preferred_element_type=F32
        )

    fill(to_mate, mate, dx_product)
    swap_dx = over_loop(to_mate, mate_dx, mate_send, mate_recv, 1)
    swap_dx.start()
    fill(dx_sum, side, dx_product)
    swap_dx.wait()
    add(dx_sum, mate_dx)
    own_out.wait()

    @pl.loop(1, n)
    def _(step):
        o_copy(step).wait()


def run_middle(send_x, send_g, w_gate, w_up, w_down):
    n, cap, part = send_x.shape
    units, width = w_gate.shape
    rows = n * cap
    vmem = pl.BlockSpec(memory_space=pltpu.VMEM)
    hbm = pl.BlockSpec(memory_space=pl.ANY)
    half = jax.ShapeDtypeStruct((n, cap, part), BF)
    full = jax.ShapeDtypeStruct((n, cap, width), BF)
    acts = jax.ShapeDtypeStruct((rows, units), BF)
    dma = pltpu.SemaphoreType.DMA
    return pl.pallas_call(
        functools.partial(middle, n),
        out_shape=(full, full, acts, acts, acts, half, half),
        in_specs=[hbm] * 5,
        out_specs=(vmem, vmem, vmem, vmem, vmem, hbm, vmem),
        scratch_shapes=[pltpu.VMEM((units, width), BF)] * 3
        + [pltpu.VMEM((rows, units), F32)] * 2
        + [pltpu.VMEM((n, cap, part), BF)] * 4
        + [dma((n,))] * 10
        + [dma((2,)), dma((2,)), dma((6,))],
        compiler_params=pltpu.CompilerParams(
            collective_id=0, has_side_effects=True, vmem_limit_bytes=61 * 1024 * 1024
        ),
        cost_estimate=pl.CostEstimate(
            flops=12 * rows * units * width, bytes_accessed=60_000_000, transcendentals=rows * units
        ),
    )(send_x, send_g, w_gate, w_up, w_down)


def shards(tokens, probs, routes, out_grad, w_gate, w_up, w_down):
    tok_count = tokens.shape[0]
    top_count = routes.shape[1]
    experts = lax.axis_size("dp")
    capacity = max(2, 3 * tok_count * top_count // (2 * experts))
    flat = routes.reshape(-1)
    count = flat.shape[0]
    labels = jnp.arange(experts, dtype=jnp.int32)
    onehot = flat[:, None] == labels[None, :]
    place = jnp.arange(count, dtype=jnp.int32)
    earlier = (place[None, :] < place[:, None]).astype(jnp.bfloat16)
    before = jnp.dot(earlier, onehot.astype(jnp.bfloat16), preferred_element_type=jnp.float32)
    rank = jnp.sum(jnp.where(onehot, before, 0.0), axis=1).astype(jnp.int32)
    target = (flat * capacity + rank).reshape(tok_count, top_count)
    slots = jnp.arange(experts * capacity, dtype=jnp.int32)
    picks = [slots[:, None] == target[:, k][None, :] for k in range(top_count)]
    pick = sum(p.astype(jnp.bfloat16) for p in picks)
    slot_prob = sum(
        jnp.sum(jnp.where(picks[k], probs[:, k][None, :], 0.0), axis=1) for k in range(top_count)
    )
    send_x = jnp.dot(pick, tokens, preferred_element_type=jnp.float32).astype(jnp.bfloat16)
    send_g = (
        jnp.dot(pick, out_grad, preferred_element_type=jnp.float32) * slot_prob[:, None]
    ).astype(jnp.bfloat16)

    def exchange(rows):
        cut = rows.reshape(experts, capacity, rows.shape[-1])
        moved = lax.all_to_all(cut, "dp", split_axis=0, concat_axis=0, tiled=True)
        return moved.reshape(experts * capacity, rows.shape[-1])

    if lax.axis_size("loop") == 2:
        shape = (experts, capacity, tokens.shape[1])
        rows_x, rows_g, hidden, dgate, dup, back_out, dx_sum = run_middle(
            send_x.reshape(shape), send_g.reshape(shape), w_gate[0], w_up[0], w_down[0]
        )
        rows_x = rows_x.reshape(experts * capacity, -1)
        rows_g = rows_g.reshape(experts * capacity, -1)
        back_out = back_out.reshape(experts * capacity, -1)
        dx_sum = dx_sum.reshape(experts * capacity, -1)
    else:
        part_x = exchange(send_x)
        part_x, send_g = lax.optimization_barrier((part_x, send_g))
        part_g = exchange(send_g)
        rows_x = lax.all_gather(part_x, "loop", axis=1, tiled=True)
        rows_g = lax.all_gather(part_g, "loop", axis=1, tiled=True)
        gate_rows = w_gate[0]
        up_rows = w_up[0]
        down_rows = w_down[0]
        contract = (((1,), (1,)), ((), ()))
        gate = lax.dot_general(rows_x, gate_rows, contract, preferred_element_type=jnp.float32)
        up = lax.dot_general(rows_x, up_rows, contract, preferred_element_type=jnp.float32)
        sig = jax.nn.sigmoid(gate)
        silu = gate * sig
        hidden = (silu * up).astype(jnp.bfloat16)
        out_part = jnp.dot(hidden, down_rows, preferred_element_type=jnp.float32)
        dhid = lax.dot_general(rows_g, down_rows, contract, preferred_element_type=jnp.float32)
        dgate = (dhid * up * sig * (1.0 + gate * (1.0 - sig))).astype(jnp.bfloat16)
        dup = (dhid * silu).astype(jnp.bfloat16)
        dx_part = jnp.dot(dgate, gate_rows, preferred_element_type=jnp.float32) + jnp.dot(
            dup, up_rows, preferred_element_type=jnp.float32
        )
        outs = lax.psum_scatter(out_part.astype(BF), "loop", scatter_dimension=1, tiled=True)
        back_out = exchange(outs)
        dx_sum = lax.psum_scatter(dx_part.astype(BF), "loop", scatter_dimension=1, tiled=True)
    back_dx = exchange(dx_sum)
    outer = (((0,), (0,)), ((), ()))
    grad_gate = lax.dot_general(dgate, rows_x, outer, preferred_element_type=jnp.float32).astype(
        jnp.bfloat16
    )[None]
    grad_up = lax.dot_general(dup, rows_x, outer, preferred_element_type=jnp.float32).astype(
        jnp.bfloat16
    )[None]
    grad_down = lax.dot_general(hidden, rows_g, outer, preferred_element_type=jnp.float32).astype(
        jnp.bfloat16
    )[None]
    wanted = [(target[:, k][:, None] == slots[None, :]) for k in range(top_count)]
    out_rows = [
        jnp.dot(w.astype(jnp.bfloat16), back_out, preferred_element_type=jnp.float32)
        for w in wanted
    ]
    layer_out = sum(probs[:, k][:, None] * out_rows[k] for k in range(top_count)).astype(
        jnp.bfloat16
    )
    grad32 = out_grad.astype(jnp.float32)
    partial_dots = jnp.stack([jnp.sum(grad32 * rows, axis=1) for rows in out_rows], axis=1)
    prob_grad = lax.psum(partial_dots, "loop")
    both = sum(w.astype(jnp.bfloat16) for w in wanted)
    input_grad = jnp.dot(both, back_dx, preferred_element_type=jnp.float32).astype(jnp.bfloat16)
    return (layer_out, input_grad, prob_grad, grad_gate, grad_up, grad_down)


def solution(mesh):
    in_specs = (
        P("dp", "loop"),
        P("dp", None),
        P("dp", None),
        P("dp", "loop"),
        P("dp", "loop", None),
        P("dp", "loop", None),
        P("dp", "loop", None),
    )
    out_specs = (
        P("dp", "loop"),
        P("dp", "loop"),
        P("dp", None),
        P("dp", "loop", None),
        P("dp", "loop", None),
        P("dp", "loop", None),
    )
    return jax.shard_map(shards, mesh=mesh, in_specs=in_specs, out_specs=out_specs, check_vma=False)
```

```python
import functools

import jax
import jax.numpy as jnp
from jax import lax
from jax.experimental import pallas as pl
from jax.experimental.pallas import tpu as pltpu
from jax.sharding import PartitionSpec as P

BF = jnp.bfloat16
F32 = jnp.float32
CONTRACT = (((1,), (1,)), ((), ()))
STEP = 256
WIDE = 512


def middle(
    n, send_x, send_g, w_gate, w_up, w_down,
    full_x, full_g, hidden, dgate, dup, back_out, dx_sum,
    wg, wu, wd, fact_gate, fact_up, out_own, to_mate, mate_out, mate_dx,
    x_out, x_in, xm_out, xm_in, g_out, g_in, gm_out, gm_in, o_out, o_in,
    mate_send, mate_recv, local_sem,
):
    me = lax.axis_index("dp")
    side = lax.axis_index("loop")
    mate = 1 - side
    cap, part = send_x.shape[1:]
    rows = n * cap
    units = wg.shape[0]
    ahead = n // 4
    mine = pl.ds(pl.multiple_of(side * part, part), part)

    def peer(step):
        return lax.rem(me + step, n)

    def source(step):
        return lax.rem(me - step + n, n)

    def over_dp(src, dst, out_sem, in_sem, step):
        return pltpu.make_async_remote_copy(
            src_ref=src, dst_ref=dst, send_sem=out_sem.at[step], recv_sem=in_sem.at[step],
            device_id={"dp": peer(step)}, device_id_type=pl.DeviceIdType.MESH,
        )

    def over_loop(src, dst, out_sem, in_sem, step):
        return pltpu.make_async_remote_copy(
            src_ref=src, dst_ref=dst, send_sem=out_sem.at[step], recv_sem=in_sem.at[step],
            device_id={"loop": mate}, device_id_type=pl.DeviceIdType.MESH,
        )

    def x_copy(step):
        return over_dp(send_x.at[peer(step)], full_x.at[me, :, mine], x_out, x_in, step)

    def g_copy(step):
        return over_dp(send_g.at[peer(step)], full_g.at[me, :, mine], g_out, g_in, step)

    def o_copy(step):
        return over_dp(out_own.at[peer(step)], back_out.at[me], o_out, o_in, step)

    def handed(full, step, out_sem, in_sem):
        at = full.at[source(step), :, mine]
        return over_loop(at, at, out_sem, in_sem, step)

    barrier = pltpu.get_barrier_semaphore()

    @pl.loop(1, n)
    def _(step):
        pl.semaphore_signal(
            barrier, inc=1, device_id={"dp": peer(step)}, device_id_type=pl.DeviceIdType.MESH
        )

    pl.semaphore_signal(
        barrier, inc=1, device_id={"loop": mate}, device_id_type=pl.DeviceIdType.MESH
    )
    pl.semaphore_wait(barrier, n)

    @pl.loop(1, n)
    def _(step):
        x_copy(step).start()

    @pl.loop(1, 1 + ahead)
    def _(step):
        g_copy(step).start()

    own_x = pltpu.make_async_copy(send_x.at[me], full_x.at[me, :, mine], local_sem.at[0])
    own_g = pltpu.make_async_copy(send_g.at[me], full_g.at[me, :, mine], local_sem.at[1])
    weights = [
        pltpu.make_async_copy(src, dst, local_sem.at[2 + i])
        for i, (src, dst) in enumerate(((w_gate, wg), (w_up, wu), (w_down, wd)))
    ]
    own_x.start()
    own_g.start()
    for copy in weights:
        copy.start()
    own_x.wait()
    own_g.wait()
    handed(full_x, 0, xm_out, xm_in).start()
    handed(full_g, 0, gm_out, gm_in).start()

    @pl.loop(1, n)
    def _(step):
        x_copy(step).wait()
        handed(full_x, step, xm_out, xm_in).start()

        @pl.when(step + ahead < n)
        def _():
            g_copy(step + ahead).start()

    for copy in weights:
        copy.wait()

    @pl.loop(0, n)
    def _(step):
        handed(full_x, step, xm_out, xm_in).wait()

    @pl.loop(0, units // STEP)
    def _(i):
        at = pl.ds(pl.multiple_of(i * STEP, STEP), STEP)
        x = full_x[...].reshape(rows, 2 * part)
        gate = lax.dot_general(x, wg[at, :], CONTRACT, preferred_element_type=F32)
        up = lax.dot_general(x, wu[at, :], CONTRACT, preferred_element_type=F32)
        sig = jax.nn.sigmoid(gate)
        silu = gate * sig
        hidden[:, at] = (silu * up).astype(BF)
        fact_up[:, at] = silu
        fact_gate[:, at] = up * sig * (1.0 + gate * (1.0 - sig))

    def fill(dst, which, product):
        @pl.loop(0, part // WIDE)
        def _(i):
            first = pl.multiple_of(i * WIDE, WIDE)
            at = pl.ds(pl.multiple_of(which * part + first, WIDE), WIDE)
            dst[:, :, pl.ds(first, WIDE)] = product(at).astype(BF).reshape(n, cap, WIDE)

    def add(dst, other):
        @pl.loop(0, n)
        def _(i):
            dst[i] = (dst[i].astype(F32) + other[i].astype(F32)).astype(BF)

    def out_product(at):
        return jnp.dot(hidden[...], wd[:, at], preferred_element_type=F32)

    fill(to_mate, mate, out_product)
    swap_out = over_loop(to_mate, mate_out, mate_send, mate_recv, 0)
    swap_out.start()
    fill(out_own, side, out_product)
    swap_out.wait()
    add(out_own, mate_out)

    @pl.loop(1, 1 + 2 * ahead)
    def _(step):
        o_copy(step).start()

    @pl.loop(1, n)
    def _(step):
        g_copy(step).wait()
        handed(full_g, step, gm_out, gm_in).start()

        @pl.when(step + 2 * ahead < n)
        def _():
            o_copy(step + 2 * ahead).start()

    own_out = pltpu.make_async_copy(out_own.at[me], back_out.at[me], local_sem.at[5])
    own_out.start()

    @pl.loop(0, n)
    def _(step):
        handed(full_g, step, gm_out, gm_in).wait()

    @pl.loop(0, units // STEP)
    def _(i):
        at = pl.ds(pl.multiple_of(i * STEP, STEP), STEP)
        g = full_g[...].reshape(rows, 2 * part)
        dhid = lax.dot_general(g, wd[at, :], CONTRACT, preferred_element_type=F32)
        dgate[:, at] = (dhid * fact_gate[:, at]).astype(BF)
        dup[:, at] = (dhid * fact_up[:, at]).astype(BF)

    def dx_product(at):
        return jnp.dot(dgate[...], wg[:, at], preferred_element_type=F32) + jnp.dot(
            dup[...], wu[:, at], preferred_element_type=F32
        )

    fill(to_mate, mate, dx_product)
    swap_dx = over_loop(to_mate, mate_dx, mate_send, mate_recv, 1)
    swap_dx.start()
    fill(dx_sum, side, dx_product)
    swap_dx.wait()
    add(dx_sum, mate_dx)
    own_out.wait()

    @pl.loop(1, n)
    def _(step):
        o_copy(step).wait()


def run_middle(send_x, send_g, w_gate, w_up, w_down):
    n, cap, part = send_x.shape
    units, width = w_gate.shape
    rows = n * cap
    vmem = pl.BlockSpec(memory_space=pltpu.VMEM)
    hbm = pl.BlockSpec(memory_space=pl.ANY)
    half = jax.ShapeDtypeStruct((n, cap, part), BF)
    full = jax.ShapeDtypeStruct((n, cap, width), BF)
    acts = jax.ShapeDtypeStruct((rows, units), BF)
    dma = pltpu.SemaphoreType.DMA
    return pl.pallas_call(
        functools.partial(middle, n),
        out_shape=(full, full, acts, acts, acts, half, half),
        in_specs=[hbm] * 5,
        out_specs=(vmem, vmem, vmem, vmem, vmem, hbm, vmem),
        scratch_shapes=[pltpu.VMEM((units, width), BF)] * 3
        + [pltpu.VMEM((rows, units), F32)] * 2
        + [pltpu.VMEM((n, cap, part), BF)] * 4
        + [dma((n,))] * 10
        + [dma((2,)), dma((2,)), dma((6,))],
        compiler_params=pltpu.CompilerParams(
            collective_id=0, has_side_effects=True, vmem_limit_bytes=61 * 1024 * 1024
        ),
        cost_estimate=pl.CostEstimate(
            flops=12 * rows * units * width, bytes_accessed=60_000_000, transcendentals=rows * units
        ),
    )(send_x, send_g, w_gate, w_up, w_down)


def shards(tokens, probs, routes, out_grad, w_gate, w_up, w_down):
    tok_count = tokens.shape[0]
    top_count = routes.shape[1]
    experts = lax.axis_size("dp")
    capacity = max(2, 3 * tok_count * top_count // (2 * experts))
    flat = routes.reshape(-1)
    count = flat.shape[0]
    labels = jnp.arange(experts, dtype=jnp.int32)
    onehot = flat[:, None] == labels[None, :]
    place = jnp.arange(count, dtype=jnp.int32)
    earlier = (place[None, :] < place[:, None]).astype(jnp.bfloat16)
    before = jnp.dot(earlier, onehot.astype(jnp.bfloat16), preferred_element_type=jnp.float32)
    rank = jnp.sum(jnp.where(onehot, before, 0.0), axis=1).astype(jnp.int32)
    target = (flat * capacity + rank).reshape(tok_count, top_count)
    slots = jnp.arange(experts * capacity, dtype=jnp.int32)
    picks = [slots[:, None] == target[:, k][None, :] for k in range(top_count)]
    pick = sum(p.astype(jnp.bfloat16) for p in picks)
    slot_prob = sum(
        jnp.sum(jnp.where(picks[k], probs[:, k][None, :], 0.0), axis=1) for k in range(top_count)
    )
    send_x = jnp.dot(pick, tokens, preferred_element_type=jnp.float32).astype(jnp.bfloat16)
    send_g = (
        jnp.dot(pick, out_grad, preferred_element_type=jnp.float32) * slot_prob[:, None]
    ).astype(jnp.bfloat16)

    def exchange(rows):
        cut = rows.reshape(experts, capacity, rows.shape[-1])
        moved = lax.all_to_all(cut, "dp", split_axis=0, concat_axis=0, tiled=True)
        return moved.reshape(experts * capacity, rows.shape[-1])

    if lax.axis_size("loop") == 2:
        shape = (experts, capacity, tokens.shape[1])
        rows_x, rows_g, hidden, dgate, dup, back_out, dx_sum = run_middle(
            send_x.reshape(shape), send_g.reshape(shape), w_gate[0], w_up[0], w_down[0]
        )
        rows_x = rows_x.reshape(experts * capacity, -1)
        rows_g = rows_g.reshape(experts * capacity, -1)
        back_out = back_out.reshape(experts * capacity, -1)
        dx_sum = dx_sum.reshape(experts * capacity, -1)
    else:
        part_x = exchange(send_x)
        part_x, send_g = lax.optimization_barrier((part_x, send_g))
        part_g = exchange(send_g)
        rows_x = lax.all_gather(part_x, "loop", axis=1, tiled=True)
        rows_g = lax.all_gather(part_g, "loop", axis=1, tiled=True)
        gate_rows = w_gate[0]
        up_rows = w_up[0]
        down_rows = w_down[0]
        contract = (((1,), (1,)), ((), ()))
        gate = lax.dot_general(rows_x, gate_rows, contract, preferred_element_type=jnp.float32)
        up = lax.dot_general(rows_x, up_rows, contract, preferred_element_type=jnp.float32)
        sig = jax.nn.sigmoid(gate)
        silu = gate * sig
        hidden = (silu * up).astype(jnp.bfloat16)
        out_part = jnp.dot(hidden, down_rows, preferred_element_type=jnp.float32)
        dhid = lax.dot_general(rows_g, down_rows, contract, preferred_element_type=jnp.float32)
        dgate = (dhid * up * sig * (1.0 + gate * (1.0 - sig))).astype(jnp.bfloat16)
        dup = (dhid * silu).astype(jnp.bfloat16)
        dx_part = jnp.dot(dgate, gate_rows, preferred_element_type=jnp.float32) + jnp.dot(
            dup, up_rows, preferred_element_type=jnp.float32
        )
        outs = lax.psum_scatter(out_part.astype(BF), "loop", scatter_dimension=1, tiled=True)
        back_out = exchange(outs)
        dx_sum = lax.psum_scatter(dx_part.astype(BF), "loop", scatter_dimension=1, tiled=True)
    back_dx = exchange(dx_sum)
    outer = (((0,), (0,)), ((), ()))
    grad_gate = lax.dot_general(dgate, rows_x, outer, preferred_element_type=jnp.float32).astype(
        jnp.bfloat16
    )[None]
    grad_up = lax.dot_general(dup, rows_x, outer, preferred_element_type=jnp.float32).astype(
        jnp.bfloat16
    )[None]
    grad_down = lax.dot_general(hidden, rows_g, outer, preferred_element_type=jnp.float32).astype(
        jnp.bfloat16
    )[None]
    wanted = [(target[:, k][:, None] == slots[None, :]) for k in range(top_count)]
    out_rows = [
        jnp.dot(w.astype(jnp.bfloat16), back_out, preferred_element_type=jnp.float32)
        for w in wanted
    ]
    layer_out = sum(probs[:, k][:, None] * out_rows[k] for k in range(top_count)).astype(
        jnp.bfloat16
    )
    grad32 = out_grad.astype(jnp.float32)
    partial_dots = jnp.stack([jnp.sum(grad32 * rows, axis=1) for rows in out_rows], axis=1)
    prob_grad = lax.psum(partial_dots, "loop")
    both = sum(w.astype(jnp.bfloat16) for w in wanted)
    input_grad = jnp.dot(both, back_dx, preferred_element_type=jnp.float32).astype(jnp.bfloat16)
    return (layer_out, input_grad, prob_grad, grad_gate, grad_up, grad_down)


def solution(mesh):
    in_specs = (
        P("dp", "loop"),
        P("dp", None),
        P("dp", None),
        P("dp", "loop"),
        P("dp", "loop", None),
        P("dp", "loop", None),
        P("dp", "loop", None),
    )
    out_specs = (
        P("dp", "loop"),
        P("dp", "loop"),
        P("dp", None),
        P("dp", "loop", None),
        P("dp", "loop", None),
        P("dp", "loop", None),
    )
    return jax.shard_map(shards, mesh=mesh, in_specs=in_specs, out_specs=out_specs, check_vma=False)
```
